32 devices in a mesh: groups: 2 (over y), seq: 4 (over z), wloop: 2 (over x), heads: 2 (over core).
Axes of the slice: x: 2, y: 2, z: 4, core: 2. Of those that a mesh axis runs over, the one named last changes fastest.
Arguments:
- activations: bfloat16 [4, 2048, 2048], P(('groups', 'wloop'), 'seq'), parts along dimension 0, may hold values from -6 to 6
- norm_gain: float32 [2048], replicated, may hold values from 0.1 to 1.9
- w_query: bfloat16 [2048, 2048], P('wloop', 'heads'), may hold values from -0.125 to 0.125
- w_keyvalue: bfloat16 [2048, 2, 2048], P('wloop', None, 'heads'), may hold values from -0.125 to 0.125
- w_output: bfloat16 [2048, 2048], P('heads', 'wloop'), may hold values from -0.125 to 0.125
- log_retain: float32 [4, 16, 2048], P(('groups', 'wloop'), 'heads', 'seq'), parts along dimension 0, may hold values from -3 to 0, as said below
- resets: int32 [4, 4], P(('groups', 'wloop'), 'seq'), parts along dimension 0, may hold values 0 or 1
Outputs:
- layer_out: bfloat16 [4, 2048, 2048], P(('groups', 'wloop'), 'seq', 'heads'), parts along dimension 0
The draws below stay inside these ranges and needn't reach their ends.
There are 2 independent parts, one for each index of `groups`. The reference program is written for one: setup_inputs(seed, part) draws one part's arguments, and reference() takes and returns one part's arrays. A program takes and returns all parts, laid end to end along the dimension named above; an argument that names none is the same for every part. Nothing has to cross between parts.
Inputs may be any that keep to these rules, and one draw needn't show every extreme that they name: `log_retain`: log retention per token and head, never above zero.
All inputs are finite; a program needn't handle non-finite values. No bound on the sum of `resets` on one device may be relied on, other than what follows from the above.
Results may differ from the reference program's by a relative error of at most 0.02.
Values may be sent and summed in bfloat16 or wider, within the bound.
A program may use at most 128 MiB of HBM per device.

```python
import math
import jax
import jax.numpy as jnp
from jax import lax

D = 2048
HEADS = 16
SEG = 512
BATCH = 2
SEGMENTS = 4
PATH_STEPS = 2048
INNER = 2048


def draw_log_retain(key, part):
    lookup_vectors = jax.random.split(key, 7)
    array_dimensions = (BATCH, HEADS, PATH_STEPS)
    fast_share = 0.5
    fast = jax.random.bernoulli(lookup_vectors[0], fast_share, (BATCH, HEADS, 1))
    fast_rate = jnp.exp(jax.random.uniform(lookup_vectors[1], (BATCH, HEADS, 1), jnp.float32, math.log(2.5), math.log(4.0))) / min(40, SEG)
    slow_rate = jnp.exp(jax.random.uniform(lookup_vectors[2], (BATCH, HEADS, 1), jnp.float32, math.log(0.1), math.log(0.5))) / PATH_STEPS
    starting_position = jnp.where(fast, fast_rate, slow_rate)
    block_fading_multiplier = jnp.exp(jax.random.uniform(lookup_vectors[3], (BATCH, HEADS, SEGMENTS, 1), jnp.float32, -math.log(2.0), math.log(2.0)))
    block_fading_multiplier = jnp.broadcast_to(block_fading_multiplier, (BATCH, HEADS, SEGMENTS, SEG)).reshape(array_dimensions)
    step_fading_multiplier = jax.random.uniform(lookup_vectors[4], array_dimensions, jnp.float32, 0.7, 1.4)
    batch_bundle = jax.random.bernoulli(lookup_vectors[5], min(0.5, 2.0 / PATH_STEPS), array_dimensions)
    bundle_count = jnp.log(jax.random.uniform(lookup_vectors[6], array_dimensions, jnp.float32, 0.67, 0.8))
    return -starting_position * block_fading_multiplier * step_fading_multiplier + jnp.where(batch_bundle, bundle_count, 0.0)


def set_ends(array, rng, least, largest):
    place = [jax.random.randint(jax.random.fold_in(rng, axis), (), 0, length) for axis, length in enumerate(array.shape)]
    widest = array.shape.index(max(array.shape))
    neighbour = place[:widest] + [(place[widest] + 1) % array.shape[widest]] + place[widest + 1:]
    return array.at[tuple(place)].set(least).at[tuple(neighbour)].set(largest)


def steps_of(rng, extent, cuts, least, top_value):
    level = 1.0
    for dim, shards_of in cuts:
        draws = jax.random.uniform(jax.random.fold_in(jax.random.fold_in(rng, 6), dim), (shards_of,), jnp.float32, least / len(cuts), top_value / len(cuts))
        level = level * jnp.repeat(jnp.exp(draws), extent[dim] // shards_of).reshape((-1,) + (1,) * (len(extent) - 1 - dim))
    return level


def centred(key, shape, scale, reach, cuts=(), kind=jnp.bfloat16):
    gain = steps_of(key, shape, cuts, -0.22, 0.18) if cuts else 1.0
    entries = jax.random.normal(key, shape, jnp.float32) * scale * gain
    return jnp.minimum(jnp.maximum(entries, -reach), reach).astype(kind)


def setup_inputs(seed: int = 0, part: int = 0) -> dict:
    streams_of = jax.random.split(jax.random.key(seed), 8)
    part_keys = jax.random.split(jax.random.fold_in(streams_of[7], part), 8)
    return {
        "activations": centred(part_keys[0], (BATCH, PATH_STEPS, D), 1.0, 6.0, ((0, 2), (1, 4))),
        "norm_gain": jnp.clip(1.0 + 0.18 * jax.random.normal(streams_of[1], (D,), jnp.float32), 0.1, 1.9),
        "w_query": centred(streams_of[2], (D, INNER), D ** -0.5, 0.125, ((0, 2), (1, 2))),
        "w_keyvalue": centred(streams_of[3], (D, 2, INNER), D ** -0.5, 0.125, ((0, 2), (2, 2))),
        "w_output": centred(streams_of[4], (INNER, D), INNER ** -0.5, 0.125, ((0, 2), (1, 2))),
        "log_retain": draw_log_retain(jax.random.fold_in(jax.random.fold_in(streams_of[7], part), 71), part),
        "resets": set_ends((jax.random.randint(part_keys[6], (BATCH, SEGMENTS), 0, 6) < 1).astype(jnp.int32), jax.random.fold_in(part_keys[6], 1), 0, 1),
    }


SCORE_SCALE = 2.0

def rms_rows(values, eps):
    return values * lax.rsqrt(lax.optimization_barrier(jnp.mean(values * values, axis=-1, keepdims=True)) + eps)

def window_block(item, scale):
    query, lookup_vectors, values, prior_keys, prior_values, allow = item
    query = query.astype(jnp.float32)
    own = jnp.einsum('ihd,jhd->hij', query, lookup_vectors.astype(jnp.float32)) * scale
    prior = jnp.einsum('ihd,jhd->hij', query, prior_keys.astype(jnp.float32)) * scale
    span = query.shape[0]
    row_pos = lax.broadcasted_iota(jnp.int32, (span, span), 0)
    column_pos = lax.broadcasted_iota(jnp.int32, (span, span), 1)
    own_w = jnp.where(column_pos <= row_pos, jnp.exp(own), 0.0)
    prior_w = jnp.where((column_pos > row_pos) & allow, jnp.exp(prior), 0.0)
    total = lax.optimization_barrier(jnp.sum(jnp.concatenate([own_w, prior_w], axis=-1), axis=-1, keepdims=True))
    own_p = (own_w / total).astype(jnp.bfloat16).astype(jnp.float32)
    prior_p = (prior_w / total).astype(jnp.bfloat16).astype(jnp.float32)
    return jnp.einsum('hij,jhd->ihd', own_p, values.astype(jnp.float32)) + jnp.einsum('hij,jhd->ihd', prior_p, prior_values.astype(jnp.float32))

def trajectory(acts, retain, reset_row, norm_gain, w_query, w_keyvalue, w_output):
    length, width = acts.shape
    heads = retain.shape[0]
    inner = w_query.shape[1]
    head_dim = inner // heads
    segments = reset_row.shape[0]
    span = length // segments
    scale = SCORE_SCALE / math.sqrt(head_dim)
    normed = (rms_rows(acts.astype(jnp.float32), 1e-05) * norm_gain).astype(jnp.bfloat16)
    query_raw = jnp.dot(normed, w_query, preferred_element_type=jnp.float32)
    key_raw = jnp.dot(normed, w_keyvalue[:, 0, :], preferred_element_type=jnp.float32)
    value_raw = jnp.dot(normed, w_keyvalue[:, 1, :], preferred_element_type=jnp.float32)
    queries = rms_rows(query_raw.reshape(segments, span, heads, head_dim), 1e-06).astype(jnp.bfloat16)
    lookup_vectors = rms_rows(key_raw.reshape(segments, span, heads, head_dim), 1e-06).astype(jnp.bfloat16)
    values = value_raw.reshape(segments, span, heads, head_dim).astype(jnp.bfloat16)
    keep = (1 - reset_row).astype(jnp.float32)
    retain_seg = retain.reshape(heads, segments, span).transpose(1, 0, 2)
    climb = jnp.cumsum(retain_seg, axis=-1)
    whole = climb[:, :, -1]
    factor = jnp.exp(whole) * keep[:, None]
    weight = jnp.exp(whole[:, :, None] - climb)
    local_state = jnp.einsum('sht,sthd,sthe->shde', weight, lookup_vectors.astype(jnp.float32), values.astype(jnp.float32), precision=lax.Precision.HIGHEST)
    local_mass = lax.optimization_barrier(jnp.sum(weight * weight, axis=-1))

    def advance(carry, item):
        state, mass = carry
        fac, add_state, add_mass = item
        return ((fac[:, None, None] * state + add_state, fac * fac * mass + add_mass), (state, mass))
    start = (jnp.zeros((heads, head_dim, head_dim), jnp.float32), jnp.zeros((heads,), jnp.float32))
    _, (entering, entering_mass) = lax.scan(advance, start, (factor, local_state, local_mass))
    entering = entering * keep[:, None, None, None]
    entering_mass = entering_mass * keep[:, None]
    read = jnp.einsum('sthd,shde->sthe', queries.astype(jnp.float32), entering, precision=lax.Precision.HIGHEST)
    read = read * jnp.exp(climb).transpose(0, 2, 1)[..., None]
    read = read / jnp.sqrt(head_dim * (1.0 + entering_mass))[:, None, :, None]
    prior_keys = jnp.concatenate([jnp.zeros_like(lookup_vectors[:1]), lookup_vectors[:-1]], axis=0)
    prior_values = jnp.concatenate([jnp.zeros_like(values[:1]), values[:-1]], axis=0)
    allow = (keep > 0.5) & (jnp.arange(segments) > 0)
    window = lax.map(lambda item: window_block(item, scale), (queries, lookup_vectors, values, prior_keys, prior_values, allow))
    attended = (window + read).astype(jnp.bfloat16).reshape(length, inner)
    mixed = jnp.dot(attended, w_output, preferred_element_type=jnp.float32)
    return (acts.astype(jnp.float32) + mixed).astype(jnp.bfloat16)

def reference(activations, norm_gain, w_query, w_keyvalue, w_output, log_retain, resets):
    return lax.map(lambda item: trajectory(item[0], item[1], item[2], norm_gain, w_query, w_keyvalue, w_output), (activations, log_retain, resets))
```

```python
import math

import jax
import jax.numpy as jnp
from jax import lax
from jax.sharding import PartitionSpec as P

SCORE_SCALE = 2.0


def shifted(value, axis, steps):
    count = lax.axis_size(axis)
    initial, last = (max(0, -steps), min(count, count - steps))
    return lax.ppermute(value, axis, [(source, source + steps) for source in range(initial, last)])


def rms_rows(values, eps):
    return values * lax.rsqrt(jnp.mean(values * values, axis=-1, keepdims=True) + eps)


def window_mix(queries, lookup_vectors, values, prior_keys, prior_values, allow, scale):
    own = (
        jnp.einsum("bihd,bjhd->bhij", queries, lookup_vectors, preferred_element_type=jnp.float32)
        * scale
    )
    prior = (
        jnp.einsum("bihd,bjhd->bhij", queries, prior_keys, preferred_element_type=jnp.float32)
        * scale
    )
    span = queries.shape[1]
    row_pos = lax.broadcasted_iota(jnp.int32, (span, span), 0)
    column_pos = lax.broadcasted_iota(jnp.int32, (span, span), 1)
    own_w = jnp.where(column_pos <= row_pos, jnp.exp(own), 0.0)
    prior_w = jnp.where((column_pos > row_pos) & allow[:, None, None, None], jnp.exp(prior), 0.0)
    total = jnp.sum(own_w, axis=-1, keepdims=True) + jnp.sum(prior_w, axis=-1, keepdims=True)
    own_p = (own_w / total).astype(jnp.bfloat16)
    prior_p = (prior_w / total).astype(jnp.bfloat16)
    return jnp.einsum(
        "bhij,bjhd->bihd", own_p, values, preferred_element_type=jnp.float32
    ) + jnp.einsum("bhij,bjhd->bihd", prior_p, prior_values, preferred_element_type=jnp.float32)


def shards(activations, norm_gain, w_query, w_keyvalue, w_output, log_retain, resets):
    trajs, span, width = activations.shape
    heads_here = log_retain.shape[1]
    inner_here = w_query.shape[1]
    head_dim = inner_here // heads_here
    scale = SCORE_SCALE / math.sqrt(head_dim)
    count = trajs * span
    normed = (rms_rows(activations.astype(jnp.float32), 1e-05) * norm_gain).astype(jnp.bfloat16)
    normed = normed.reshape(count, width)
    columns = normed
    query_raw = jnp.dot(
        columns,
        lax.all_gather(w_query, "wloop", axis=0, tiled=True),
        preferred_element_type=jnp.float32,
    )
    columns = normed
    pair_raw = jnp.einsum(
        "td,dje->jte",
        columns,
        lax.all_gather(w_keyvalue, "wloop", axis=0, tiled=True),
        preferred_element_type=jnp.float32,
    )
    lookup_vectors = rms_rows(pair_raw[0].reshape(trajs, span, heads_here, head_dim), 1e-06).astype(
        jnp.bfloat16
    )
    values = pair_raw[1].reshape(trajs, span, heads_here, head_dim).astype(jnp.bfloat16)
    prior_keys, prior_values = shifted(
        (lookup_vectors.reshape(trajs, span, inner_here), values.reshape(trajs, span, inner_here)),
        "seq",
        1,
    )
    queries = rms_rows(query_raw.reshape(trajs, span, heads_here, head_dim), 1e-06).astype(
        jnp.bfloat16
    )
    keep = (1 - resets[:, 0]).astype(jnp.float32)
    upto = jnp.triu(jnp.ones((span, span), jnp.float32))
    climb = jnp.dot(log_retain.reshape(trajs * heads_here, span), upto, precision=lax.Precision.HIGHEST)
    climb = climb.reshape(trajs, heads_here, span)
    whole = climb[:, :, -1]
    factor = jnp.exp(whole) * keep[:, None]
    weight = jnp.exp(whole[:, :, None] - climb)
    local_state = jnp.einsum(
        "bht,bthd,bthe->bhde",
        weight,
        lookup_vectors.astype(jnp.float32),
        values.astype(jnp.float32),
        precision=lax.Precision.HIGHEST,
    )
    local_mass = jnp.sum(weight * weight, axis=-1)

    def relay_turn(turn, carry):
        state, mass = carry
        return (
            shifted(
                (factor[:, :, None, None] * state + local_state).astype(jnp.bfloat16), "seq", 1
            ).astype(jnp.float32),
            shifted((factor * factor * mass + local_mass).astype(jnp.bfloat16), "seq", 1).astype(
                jnp.float32
            ),
        )

    entering, entering_mass = lax.fori_loop(
        0,
        lax.axis_size("seq") - 1,
        relay_turn,
        (jnp.zeros_like(local_state), jnp.zeros_like(local_mass)),
    )
    entering = entering * keep[:, None, None, None]
    entering_mass = entering_mass * keep[:, None]
    read = jnp.einsum(
        "bthd,bhde->bthe", queries.astype(jnp.float32), entering, precision=lax.Precision.HIGHEST
    )
    read = read * jnp.exp(climb).transpose(0, 2, 1)[..., None]
    read = read / jnp.sqrt(head_dim * (1.0 + entering_mass))[:, None, :, None]
    allow = (keep > 0.5) & (lax.axis_index("seq") > 0)
    window = window_mix(
        queries,
        lookup_vectors,
        values,
        prior_keys.reshape(trajs, span, heads_here, head_dim),
        prior_values.reshape(trajs, span, heads_here, head_dim),
        allow,
        scale,
    )
    attended = (window + read).astype(jnp.bfloat16).reshape(count, inner_here)
    partial_out = jnp.dot(
        attended,
        lax.all_gather(w_output, "wloop", axis=1, tiled=True),
        preferred_element_type=jnp.float32,
    )
    summed = lax.psum_scatter(
        partial_out.astype(jnp.bfloat16), "heads", scatter_dimension=1, tiled=True
    ).astype(jnp.float32)
    share = summed.shape[1]
    residual = lax.dynamic_slice_in_dim(
        activations.reshape(count, width), lax.axis_index("heads") * share, share, 1
    )
    return (residual.astype(jnp.float32) + summed).astype(jnp.bfloat16).reshape(trajs, span, share)


def solution(mesh):
    placed = (
        P(("groups", "wloop"), "seq", None),
        P(),
        P("wloop", "heads"),
        P("wloop", None, "heads"),
        P("heads", "wloop"),
        P(("groups", "wloop"), "heads", "seq"),
        P(("groups", "wloop"), "seq"),
    )
    return jax.shard_map(
        shards,
        mesh=mesh,
        in_specs=placed,
        out_specs=P(("groups", "wloop"), "seq", "heads"),
        check_vma=False,
    )
```

```python
import functools
import math

import jax
import jax.numpy as jnp
from jax import lax
from jax.experimental import pallas as pl
from jax.experimental.pallas import tpu as pltpu
from jax.sharding import PartitionSpec as P

SCORE_SCALE = 2.0
F32, BF16 = jnp.float32, jnp.bfloat16


def around(value, axis):
    count = lax.axis_size(axis)
    return lax.ppermute(value, axis, [(i, (i + 1) % count) for i in range(count)])


def shifted(value, axis):
    count = lax.axis_size(axis)
    return lax.ppermute(value, axis, [(i, i + 1) for i in range(count - 1)])


def rms_rows(values, eps):
    return values * lax.rsqrt(jnp.mean(values * values, axis=-1, keepdims=True) + eps)


def other_half(block):
    group = lax.axis_index("groups")
    rows = block.shape[0] // 2
    first = around(lax.dynamic_slice_in_dim(block, group * rows, rows, 0), "wloop")
    second = around(first, "groups")
    return jnp.concatenate(
        [jnp.where(group == 0, first, second), jnp.where(group == 0, second, first)], axis=0
    )


def window_kernel(scale, allow_ref, q_ref, k_ref, v_ref, out_ref):
    span = q_ref.shape[0]
    query = q_ref[...]
    product = functools.partial(
        lax.dot_general, dimension_numbers=(((1,), (1,)), ((), ())), preferred_element_type=F32
    )
    prior = product(query, k_ref[:span, :])
    own = product(query, k_ref[span:, :])
    lower = lax.broadcasted_iota(jnp.int32, (span, span), 1) <= lax.broadcasted_iota(
        jnp.int32, (span, span), 0
    )
    weight = jnp.exp(jnp.where(lower, own, prior) * scale)
    own_w = jnp.where(lower, weight, 0.0)
    prior_w = jnp.where(lower, 0.0, weight) * allow_ref[0, 0]
    total = jnp.sum(own_w + prior_w, axis=-1, keepdims=True)
    mixed = jnp.dot(own_w.astype(BF16), v_ref[span:, :], preferred_element_type=F32)
    mixed += jnp.dot(prior_w.astype(BF16), v_ref[:span, :], preferred_element_type=F32)
    out_ref[...] = mixed / total


def window_mix(queries, keys, values, allow, head_dim, scale):
    span, inner = queries.shape
    return pl.pallas_call(
        functools.partial(window_kernel, scale),
        grid=(inner // head_dim,),
        in_specs=[
            pl.BlockSpec(memory_space=pltpu.SMEM),
            pl.BlockSpec((span, head_dim), lambda h: (0, h)),
            pl.BlockSpec((2 * span, head_dim), lambda h: (0, h)),
            pl.BlockSpec((2 * span, head_dim), lambda h: (0, h)),
        ],
        out_specs=pl.BlockSpec((span, head_dim), lambda h: (0, h)),
        out_shape=jax.ShapeDtypeStruct((span, inner), F32),
        compiler_params=pltpu.CompilerParams(vmem_limit_bytes=32 << 20),
        cost_estimate=pl.CostEstimate(
            flops=8 * span * span * inner, bytes_accessed=14 * span * inner, transcendentals=0
        ),
    )(allow, queries, keys, values)


def read_kernel(q_ref, state_ref, decay_ref, window_ref, out_ref):
    head = pl.program_id(0)
    decay = decay_ref[...]
    column = lax.broadcasted_iota(jnp.int32, decay.shape, 1)
    mine = jnp.sum(jnp.where(column == head, decay, 0.0), axis=-1, keepdims=True)
    read = jnp.dot(q_ref[...], state_ref[0], preferred_element_type=F32)
    out_ref[...] = (window_ref[...] + mine * read).astype(BF16)


def add_read(queries, states, decay, window):
    span, inner = queries.shape
    heads, head_dim = states.shape[:2]
    block = pl.BlockSpec((span, head_dim), lambda h: (0, h))
    return pl.pallas_call(
        read_kernel,
        grid=(heads,),
        in_specs=[
            block,
            pl.BlockSpec((1, head_dim, head_dim), lambda h: (h, 0, 0)),
            pl.BlockSpec((span, heads), lambda h: (0, 0)),
            block,
        ],
        out_specs=block,
        out_shape=jax.ShapeDtypeStruct((span, inner), BF16),
    )(queries, states, decay, window)


def shards(activations, norm_gain, w_query, w_keyvalue, w_output, log_retain, resets):
    trajs, span, width = activations.shape
    heads_here = log_retain.shape[1]
    inner_here = w_query.shape[1]
    head_dim = inner_here // heads_here
    scale = SCORE_SCALE / math.sqrt(head_dim)
    side, core, seg = lax.axis_index("wloop"), lax.axis_index("heads"), lax.axis_index("seq")
    segments = lax.axis_size("seq")
    paired = lax.axis_size("wloop") == 2 and lax.axis_size("groups") == 2
    acts = activations.reshape(span, width)

    def whole_rows(block):
        if not paired:
            return lax.all_gather(block, "wloop", axis=0, tiled=True)
        other = other_half(block)
        return jnp.concatenate(
            [jnp.where(side == 0, block, other), jnp.where(side == 0, other, block)], axis=0
        )

    normed = (rms_rows(acts.astype(F32), 1e-05) * norm_gain).astype(BF16)
    both = jnp.concatenate([shifted(normed, "seq"), normed], axis=0)
    w_key, w_value = w_keyvalue[:, 0, :], w_keyvalue[:, 1, :]
    w_key, w_value, w_query = whole_rows(w_key), whole_rows(w_value), whole_rows(w_query)

    def headed(raw):
        return rms_rows(raw.reshape(-1, heads_here, head_dim), 1e-06).astype(BF16)

    keys = headed(jnp.dot(both, w_key, preferred_element_type=F32)).reshape(2 * span, inner_here)
    values = jnp.dot(both, w_value, preferred_element_type=F32).astype(BF16)
    queries = headed(jnp.dot(normed, w_query, preferred_element_type=F32)).reshape(span, inner_here)

    keep = (1 - resets[0, 0]).astype(F32)
    upto = jnp.triu(jnp.ones((span, span), F32))
    climb = jnp.dot(log_retain[0], upto, precision=lax.Precision.HIGHEST)
    whole = climb[:, -1]
    factor = jnp.exp(whole) * keep
    weight = jnp.exp(whole[:, None] - climb)
    faded = (
        keys[span:].reshape(span, heads_here, head_dim).astype(F32) * weight.T[:, :, None]
    ).astype(BF16)
    local_state = jnp.einsum(
        "thd,the->hde",
        faded,
        values[span:].reshape(span, heads_here, head_dim),
        preferred_element_type=F32,
    )
    local_mass = jnp.sum(weight * weight, axis=-1)
    states = lax.all_gather(local_state.astype(BF16), "seq")
    small = lax.all_gather(jnp.stack([factor, local_mass]), "seq")
    state, mass = jnp.zeros_like(local_state), jnp.zeros_like(local_mass)
    for j in range(segments - 1):
        fac, add_mass = small[j, 0], small[j, 1]
        past = j < seg
        state = jnp.where(past, fac[:, None, None] * state + states[j].astype(F32), state)
        mass = jnp.where(past, fac * fac * mass + add_mass, mass)
    entering = (state * keep).astype(BF16)
    decay = jnp.exp(climb) / jnp.sqrt(head_dim * (1.0 + mass * keep))[:, None]
    allow = ((keep > 0.5) & (seg > 0)).astype(F32).reshape(1, 1)
    window = window_mix(queries, keys, values, allow, head_dim, scale)
    attended = add_read(queries, entering, decay.T, window)

    if paired:
        other = other_half(w_output)
        mine = jnp.where(side == core, w_output, other)
        theirs = jnp.where(side == core, other, w_output)
    else:
        full = lax.all_gather(w_output, "wloop", axis=1, tiled=True)
        share = width // 2
        mine = lax.dynamic_slice_in_dim(full, core * share, share, 1)
        theirs = lax.dynamic_slice_in_dim(full, (1 - core) * share, share, 1)
    sent = around(jnp.dot(attended, theirs, preferred_element_type=F32).astype(BF16), "heads")
    share = mine.shape[1]
    summed = jnp.dot(attended, mine, preferred_element_type=F32) + sent.astype(F32)
    residual = lax.dynamic_slice_in_dim(acts, core * share, share, 1)
    return (residual.astype(F32) + summed).astype(BF16).reshape(trajs, span, share)


def solution(mesh):
    placed = (
        P(("groups", "wloop"), "seq", None),
        P(),
        P("wloop", "heads"),
        P("wloop", None, "heads"),
        P("heads", "wloop"),
        P(("groups", "wloop"), "heads", "seq"),
        P(("groups", "wloop"), "seq"),
    )
    return jax.shard_map(
        shards,
        mesh=mesh,
        in_specs=placed,
        out_specs=P(("groups", "wloop"), "seq", "heads"),
        check_vma=False,
    )
```

```python
import functools
import math

import jax
import jax.numpy as jnp
from jax import lax
from jax.experimental import pallas as pl
from jax.experimental.pallas import tpu as pltpu
from jax.sharding import PartitionSpec as P

SCORE_SCALE = 2.0
F32, BF16 = jnp.float32, jnp.bfloat16


def around(value, axis):
    count = lax.axis_size(axis)
    return lax.ppermute(value, axis, [(i, (i + 1) % count) for i in range(count)])


def shifted(value, axis):
    count = lax.axis_size(axis)
    return lax.ppermute(value, axis, [(i, i + 1) for i in range(count - 1)])


def rms_rows(values, eps):
    return values * lax.rsqrt(jnp.mean(values * values, axis=-1, keepdims=True) + eps)


def after(value, *earlier):
    return lax.optimization_barrier((value, *earlier))[0]


def rows_of_group(block):
    rows = block.shape[0] // 2
    return lax.dynamic_slice_in_dim(block, lax.axis_index("groups") * rows, rows, 0)


def projection_kernel(head_dim, place_ref, x_ref, own_ref, first_ref, second_ref, out_ref):
    side, group = place_ref[0], place_ref[1]
    deep, part = own_ref.shape[0], first_ref.shape[0]

    def columns(start, size):
        return x_ref[:, pl.ds(pl.multiple_of(start, 128), size)]

    total = jnp.dot(columns(side * deep, deep), own_ref[...], preferred_element_type=F32)
    base = (1 - side) * deep
    total += jnp.dot(columns(base + group * part, part), first_ref[...], preferred_element_type=F32)
    total += jnp.dot(
        columns(base + (1 - group) * part, part), second_ref[...], preferred_element_type=F32
    )
    if not head_dim:
        out_ref[...] = total.astype(BF16)
        return
    for start in range(0, total.shape[1], head_dim):
        head = total[:, start : start + head_dim]
        out_ref[:, start : start + head_dim] = rms_rows(head, 1e-06).astype(BF16)


def projection(place, rows, own, first, second, head_dim):
    count, width = rows.shape
    inner = own.shape[1]
    tile = 256
    return pl.pallas_call(
        functools.partial(projection_kernel, head_dim),
        grid=(inner // tile,),
        in_specs=[
            pl.BlockSpec(memory_space=pltpu.SMEM),
            pl.BlockSpec((count, width), lambda c: (0, 0)),
            pl.BlockSpec((own.shape[0], tile), lambda c: (0, c)),
            pl.BlockSpec((first.shape[0], tile), lambda c: (0, c)),
            pl.BlockSpec((second.shape[0], tile), lambda c: (0, c)),
        ],
        out_specs=pl.BlockSpec((count, tile), lambda c: (0, c)),
        out_shape=jax.ShapeDtypeStruct((count, inner), BF16),
        compiler_params=pltpu.CompilerParams(vmem_limit_bytes=32 << 20),
        cost_estimate=pl.CostEstimate(
            flops=2 * count * width * inner,
            bytes_accessed=2 * (count * width + width * inner + count * inner),
            transcendentals=0,
        ),
    )(place, rows, own, first, second)


def state_kernel(k_ref, v_ref, weight_ref, out_ref):
    head = pl.program_id(0)
    weight = weight_ref[...]
    column = lax.broadcasted_iota(jnp.int32, weight.shape, 1)
    mine = jnp.sum(jnp.where(column == head, weight, 0.0), axis=-1, keepdims=True)
    faded = (k_ref[...].astype(F32) * mine).astype(BF16)
    out_ref[0] = lax.dot_general(
        faded, v_ref[...], (((0,), (0,)), ((), ())), preferred_element_type=F32
    ).astype(BF16)


def local_states(keys, values, weight, head_dim):
    span, heads = weight.shape
    block = pl.BlockSpec((span, head_dim), lambda h: (1, h))
    return pl.pallas_call(
        state_kernel,
        grid=(heads,),
        in_specs=[block, block, pl.BlockSpec((span, heads), lambda h: (0, 0))],
        out_specs=pl.BlockSpec((1, head_dim, head_dim), lambda h: (h, 0, 0)),
        out_shape=jax.ShapeDtypeStruct((heads, head_dim, head_dim), BF16),
    )(keys, values, weight)


def two_parts(value):
    high = value.astype(BF16)
    return high, (value - high.astype(F32)).astype(BF16)


def window_kernel(scale, allow_ref, q_ref, k_ref, v_ref, out_ref):
    span = q_ref.shape[0]
    query = q_ref[...]
    product = functools.partial(
        lax.dot_general, dimension_numbers=(((1,), (1,)), ((), ())), preferred_element_type=F32
    )
    prior = product(query, k_ref[:span, :])
    own = product(query, k_ref[span:, :])
    lower = lax.broadcasted_iota(jnp.int32, (span, span), 1) <= lax.broadcasted_iota(
        jnp.int32, (span, span), 0
    )
    weight = jnp.exp(jnp.where(lower, own, prior) * scale)
    own_w = jnp.where(lower, weight, 0.0)
    prior_w = jnp.where(lower, 0.0, weight) * allow_ref[0, 0]
    total = jnp.sum(own_w + prior_w, axis=-1, keepdims=True)
    mixed = jnp.dot(own_w.astype(BF16), v_ref[span:, :], preferred_element_type=F32)
    mixed += jnp.dot(prior_w.astype(BF16), v_ref[:span, :], preferred_element_type=F32)
    out_ref[...] = mixed / total


def window_mix(queries, keys, values, allow, head_dim, scale):
    span, inner = queries.shape
    return pl.pallas_call(
        functools.partial(window_kernel, scale),
        grid=(inner // head_dim,),
        in_specs=[
            pl.BlockSpec(memory_space=pltpu.SMEM),
            pl.BlockSpec((span, head_dim), lambda h: (0, h)),
            pl.BlockSpec((2 * span, head_dim), lambda h: (0, h)),
            pl.BlockSpec((2 * span, head_dim), lambda h: (0, h)),
        ],
        out_specs=pl.BlockSpec((span, head_dim), lambda h: (0, h)),
        out_shape=jax.ShapeDtypeStruct((span, inner), F32),
        compiler_params=pltpu.CompilerParams(vmem_limit_bytes=32 << 20),
        cost_estimate=pl.CostEstimate(
            flops=8 * span * span * inner, bytes_accessed=14 * span * inner, transcendentals=0
        ),
    )(allow, queries, keys, values)


def read_kernel(q_ref, state_ref, decay_ref, window_ref, out_ref):
    head = pl.program_id(0)
    decay = decay_ref[...]
    column = lax.broadcasted_iota(jnp.int32, decay.shape, 1)
    mine = jnp.sum(jnp.where(column == head, decay, 0.0), axis=-1, keepdims=True)
    read = jnp.dot(q_ref[...], state_ref[0], preferred_element_type=F32)
    out_ref[...] = (window_ref[...] + mine * read).astype(BF16)


def add_read(queries, states, decay, window):
    span, inner = queries.shape
    heads, head_dim = states.shape[:2]
    block = pl.BlockSpec((span, head_dim), lambda h: (0, h))
    return pl.pallas_call(
        read_kernel,
        grid=(heads,),
        in_specs=[
            block,
            pl.BlockSpec((1, head_dim, head_dim), lambda h: (h, 0, 0)),
            pl.BlockSpec((span, heads), lambda h: (0, 0)),
            block,
        ],
        out_specs=block,
        out_shape=jax.ShapeDtypeStruct((span, inner), BF16),
    )(queries, states, decay, window)


def shards(activations, norm_gain, w_query, w_keyvalue, w_output, log_retain, resets):
    trajs, span, width = activations.shape
    heads_here = log_retain.shape[1]
    inner_here = w_query.shape[1]
    head_dim = inner_here // heads_here
    scale = SCORE_SCALE / math.sqrt(head_dim)
    side, core, seg = lax.axis_index("wloop"), lax.axis_index("heads"), lax.axis_index("seq")
    segments = lax.axis_size("seq")
    paired = lax.axis_size("wloop") == 2 and lax.axis_size("groups") == 2
    acts = activations.reshape(span, width)

    place = jnp.stack([side, lax.axis_index("groups")]).astype(jnp.int32)
    w_pair = w_keyvalue.reshape(w_keyvalue.shape[0], 2 * inner_here)
    own = [w_pair[:, :inner_here], w_pair[:, inner_here:], w_query, w_output]
    if paired:
        firsts, seconds = [], []
        for block in own:
            part = rows_of_group(block)
            if firsts:
                part = after(part, firsts[-1])
            firsts.append(around(part, "wloop"))
            part = firsts[-1]
            if seconds:
                part = after(part, seconds[-1])
            seconds.append(around(part, "groups"))
        blocks = list(zip(own, firsts, seconds))
    else:
        place = jnp.zeros((2,), jnp.int32)
        blocks = []
        for block in own[:3]:
            full = lax.all_gather(block, "wloop", axis=0, tiled=True)
            half = full.shape[0] // 2
            blocks.append((full[:half], full[half : half + half // 2], full[half + half // 2 :]))

    normed = (rms_rows(acts.astype(F32), 1e-05) * norm_gain).astype(BF16)
    lane = width // 2
    ours = shifted(lax.dynamic_slice_in_dim(normed, core * lane, lane, 1), "seq")
    theirs = around(ours, "heads")
    prior = jnp.concatenate(
        [jnp.where(core == 0, ours, theirs), jnp.where(core == 0, theirs, ours)], axis=1
    )
    both = jnp.concatenate([prior, normed], axis=0)
    keys = projection(place, both, *blocks[0], head_dim)
    values = projection(place, both, *blocks[1], 0)
    queries = projection(place, normed, *blocks[2], head_dim)

    keep = (1 - resets[0, 0]).astype(F32)
    upto = jnp.triu(jnp.ones((span, span), F32))
    climb = jnp.dot(log_retain[0], upto, precision=lax.Precision.HIGHEST)
    whole = climb[:, -1]
    factor = jnp.exp(whole) * keep
    weight = jnp.exp(whole[:, None] - climb)
    local_state = local_states(keys, values, weight.T, head_dim)
    small = jnp.stack([*two_parts(factor), *two_parts(jnp.sum(weight * weight, axis=-1))], axis=1)
    small = jnp.pad(small, ((0, 0), (0, 12)))
    small = jnp.broadcast_to(small[:, :, None], (heads_here, 16, head_dim))
    gathered = lax.all_gather(jnp.concatenate([local_state, small], axis=1), "seq")
    state, mass = jnp.zeros(local_state.shape, F32), jnp.zeros(factor.shape, F32)
    for j in range(segments - 1):
        tail = gathered[j, :, head_dim : head_dim + 4, 0].astype(F32)
        fac, add_mass = tail[:, 0] + tail[:, 1], tail[:, 2] + tail[:, 3]
        past = j < seg
        local = gathered[j, :, :head_dim].astype(F32)
        state = jnp.where(past, fac[:, None, None] * state + local, state)
        mass = jnp.where(past, fac * fac * mass + add_mass, mass)
    entering = (state * keep).astype(BF16)
    decay = jnp.exp(climb) / jnp.sqrt(head_dim * (1.0 + mass * keep))[:, None]
    allow = ((keep > 0.5) & (seg > 0)).astype(F32).reshape(1, 1)
    window = window_mix(queries, keys, values, allow, head_dim, scale)
    attended = add_read(queries, entering, decay.T, window)

    if paired:
        first, second = blocks[3][1:]
        group = lax.axis_index("groups")
        other = jnp.concatenate(
            [jnp.where(group == 0, first, second), jnp.where(group == 0, second, first)], axis=0
        )
        mine = jnp.where(side == core, w_output, other)
        theirs = jnp.where(side == core, other, w_output)
    else:
        full = lax.all_gather(w_output, "wloop", axis=1, tiled=True)
        share = width // 2
        mine = lax.dynamic_slice_in_dim(full, core * share, share, 1)
        theirs = lax.dynamic_slice_in_dim(full, (1 - core) * share, share, 1)
    sent = around(jnp.dot(attended, theirs, preferred_element_type=F32).astype(BF16), "heads")
    share = mine.shape[1]
    summed = jnp.dot(attended, mine, preferred_element_type=F32) + sent.astype(F32)
    residual = lax.dynamic_slice_in_dim(acts, core * share, share, 1)
    return (residual.astype(F32) + summed).astype(BF16).reshape(trajs, span, share)


def solution(mesh):
    placed = (
        P(("groups", "wloop"), "seq", None),
        P(),
        P("wloop", "heads"),
        P("wloop", None, "heads"),
        P("heads", "wloop"),
        P(("groups", "wloop"), "heads", "seq"),
        P(("groups", "wloop"), "seq"),
    )
    return jax.shard_map(
        shards,
        mesh=mesh,
        in_specs=placed,
        out_specs=P(("groups", "wloop"), "seq", "heads"),
        check_vma=False,
    )
```

```python
import functools
import math

import jax
import jax.numpy as jnp
from jax import lax
from jax.experimental import pallas as pl
from jax.experimental.pallas import tpu as pltpu
from jax.sharding import PartitionSpec as P

SCORE_SCALE = 2.0
F32, BF16 = jnp.float32, jnp.bfloat16


def around(value, axis):
    count = lax.axis_size(axis)
    return lax.ppermute(value, axis, [(i, (i + 1) % count) for i in range(count)])


def shifted(value, axis):
    count = lax.axis_size(axis)
    return lax.ppermute(value, axis, [(i, i + 1) for i in range(count - 1)])


def rms_rows(values, eps):
    return values * lax.rsqrt(jnp.mean(values * values, axis=-1, keepdims=True) + eps)


def after(value, *earlier):
    return lax.optimization_barrier((value, *earlier))[0]


def part_of(block, index, count):
    rows = block.shape[0] // count
    return lax.dynamic_slice_in_dim(block, index * rows, rows, 0)


def swapped(value, axis):
    count = lax.axis_size(axis)
    return lax.ppermute(value, axis, [(i, i + 1 - 2 * (i % 2)) for i in range(count)])


def in_order(index, first, second):
    return jnp.concatenate(
        [jnp.where(index == 0, first, second), jnp.where(index == 0, second, first)], axis=0
    )


def projection_kernel(head_dim, place_ref, x_ref, own_ref, first_ref, second_ref, out_ref):
    side, group = place_ref[0], place_ref[1]
    deep, part = own_ref.shape[0], first_ref.shape[0]

    def columns(start, size):
        return x_ref[:, pl.ds(pl.multiple_of(start, 128), size)]

    total = jnp.dot(columns(side * deep, deep), own_ref[...], preferred_element_type=F32)
    base = (1 - side) * deep
    total += jnp.dot(columns(base + group * part, part), first_ref[...], preferred_element_type=F32)
    total += jnp.dot(
        columns(base + (1 - group) * part, part), second_ref[...], preferred_element_type=F32
    )
    if not head_dim:
        out_ref[...] = total.astype(BF16)
        return
    for start in range(0, total.shape[1], head_dim):
        head = total[:, start : start + head_dim]
        out_ref[:, start : start + head_dim] = rms_rows(head, 1e-06).astype(BF16)


def projection(place, rows, own, first, second, head_dim):
    count, width = rows.shape
    inner = own.shape[1]
    tile = 256
    return pl.pallas_call(
        functools.partial(projection_kernel, head_dim),
        grid=(inner // tile,),
        in_specs=[
            pl.BlockSpec(memory_space=pltpu.SMEM),
            pl.BlockSpec((count, width), lambda c: (0, 0)),
            pl.BlockSpec((own.shape[0], tile), lambda c: (0, c)),
            pl.BlockSpec((first.shape[0], tile), lambda c: (0, c)),
            pl.BlockSpec((second.shape[0], tile), lambda c: (0, c)),
        ],
        out_specs=pl.BlockSpec((count, tile), lambda c: (0, c)),
        out_shape=jax.ShapeDtypeStruct((count, inner), BF16),
        compiler_params=pltpu.CompilerParams(vmem_limit_bytes=32 << 20),
        cost_estimate=pl.CostEstimate(
            flops=2 * count * width * inner,
            bytes_accessed=2 * (count * width + width * inner + count * inner),
            transcendentals=0,
        ),
    )(place, rows, own, first, second)


def state_kernel(k_ref, v_ref, weight_ref, out_ref):
    head = pl.program_id(0)
    weight = weight_ref[...]
    column = lax.broadcasted_iota(jnp.int32, weight.shape, 1)
    mine = jnp.sum(jnp.where(column == head, weight, 0.0), axis=-1, keepdims=True)
    faded = (k_ref[...].astype(F32) * mine).astype(BF16)
    out_ref[0] = lax.dot_general(
        faded, v_ref[...], (((0,), (0,)), ((), ())), preferred_element_type=F32
    ).astype(BF16)


def local_states(keys, values, weight, head_dim):
    span, heads = weight.shape
    block = pl.BlockSpec((span, head_dim), lambda h: (1, h))
    return pl.pallas_call(
        state_kernel,
        grid=(heads,),
        in_specs=[block, block, pl.BlockSpec((span, heads), lambda h: (0, 0))],
        out_specs=pl.BlockSpec((1, head_dim, head_dim), lambda h: (h, 0, 0)),
        out_shape=jax.ShapeDtypeStruct((heads, head_dim, head_dim), BF16),
    )(keys, values, weight)


def two_parts(value):
    high = value.astype(BF16)
    return high, (value - high.astype(F32)).astype(BF16)


def window_kernel(scale, allow_ref, q_ref, k_ref, v_ref, out_ref):
    span = q_ref.shape[0]
    query = q_ref[...]
    product = functools.partial(
        lax.dot_general, dimension_numbers=(((1,), (1,)), ((), ())), preferred_element_type=F32
    )
    prior = product(query, k_ref[:span, :])
    own = product(query, k_ref[span:, :])
    lower = lax.broadcasted_iota(jnp.int32, (span, span), 1) <= lax.broadcasted_iota(
        jnp.int32, (span, span), 0
    )
    weight = jnp.exp(jnp.where(lower, own, prior) * scale)
    own_w = jnp.where(lower, weight, 0.0)
    prior_w = jnp.where(lower, 0.0, weight) * allow_ref[0, 0]
    total = jnp.sum(own_w + prior_w, axis=-1, keepdims=True)
    mixed = jnp.dot(own_w.astype(BF16), v_ref[span:, :], preferred_element_type=F32)
    mixed += jnp.dot(prior_w.astype(BF16), v_ref[:span, :], preferred_element_type=F32)
    out_ref[...] = mixed / total


def window_mix(queries, keys, values, allow, head_dim, scale):
    span, inner = queries.shape
    return pl.pallas_call(
        functools.partial(window_kernel, scale),
        grid=(inner // head_dim,),
        in_specs=[
            pl.BlockSpec(memory_space=pltpu.SMEM),
            pl.BlockSpec((span, head_dim), lambda h: (0, h)),
            pl.BlockSpec((2 * span, head_dim), lambda h: (0, h)),
            pl.BlockSpec((2 * span, head_dim), lambda h: (0, h)),
        ],
        out_specs=pl.BlockSpec((span, head_dim), lambda h: (0, h)),
        out_shape=jax.ShapeDtypeStruct((span, inner), F32),
        compiler_params=pltpu.CompilerParams(vmem_limit_bytes=32 << 20),
        cost_estimate=pl.CostEstimate(
            flops=8 * span * span * inner, bytes_accessed=14 * span * inner, transcendentals=0
        ),
    )(allow, queries, keys, values)


def read_kernel(q_ref, state_ref, decay_ref, window_ref, out_ref):
    head = pl.program_id(0)
    decay = decay_ref[...]
    column = lax.broadcasted_iota(jnp.int32, decay.shape, 1)
    mine = jnp.sum(jnp.where(column == head, decay, 0.0), axis=-1, keepdims=True)
    read = jnp.dot(q_ref[...], state_ref[0], preferred_element_type=F32)
    out_ref[...] = (window_ref[...] + mine * read).astype(BF16)


def add_read(queries, states, decay, window):
    span, inner = queries.shape
    heads, head_dim = states.shape[:2]
    block = pl.BlockSpec((span, head_dim), lambda h: (0, h))
    return pl.pallas_call(
        read_kernel,
        grid=(heads,),
        in_specs=[
            block,
            pl.BlockSpec((1, head_dim, head_dim), lambda h: (h, 0, 0)),
            pl.BlockSpec((span, heads), lambda h: (0, 0)),
            block,
        ],
        out_specs=block,
        out_shape=jax.ShapeDtypeStruct((span, inner), BF16),
    )(queries, states, decay, window)


def shards(activations, norm_gain, w_query, w_keyvalue, w_output, log_retain, resets):
    trajs, span, width = activations.shape
    heads_here = log_retain.shape[1]
    inner_here = w_query.shape[1]
    head_dim = inner_here // heads_here
    scale = SCORE_SCALE / math.sqrt(head_dim)
    side, core, seg = lax.axis_index("wloop"), lax.axis_index("heads"), lax.axis_index("seq")
    segments = lax.axis_size("seq")
    paired = lax.axis_size("wloop") == 2 and lax.axis_size("groups") == 2
    paired = paired and segments % 2 == 0
    acts = activations.reshape(span, width)

    group, twin = lax.axis_index("groups"), seg % 2
    place = jnp.stack([side, group]).astype(jnp.int32)
    place_query = jnp.stack([side, twin]).astype(jnp.int32)
    normed = (rms_rows(acts.astype(F32), 1e-05) * norm_gain).astype(BF16)
    lane = width // 2
    ours = shifted(lax.dynamic_slice_in_dim(normed, core * lane, lane, 1), "seq")
    w_pair = w_keyvalue.reshape(w_keyvalue.shape[0], 2 * inner_here)
    own = [w_pair[:, :inner_here], w_pair[:, inner_here:], w_query, w_output]
    if paired:
        key_x = swapped(part_of(own[0], group, 2), "wloop")
        key_y = swapped(key_x, "groups")
        value_x = swapped(after(part_of(own[1], 2 * group + twin, 4), key_x), "wloop")
        query_x = swapped(after(part_of(own[2], twin, 2), value_x), "wloop")
        value_z = swapped(after(value_x, ours), "seq")
        value_half = in_order(twin, value_x, value_z)
        value_y = swapped(after(value_half, key_y), "groups")
        output_x = swapped(after(part_of(own[3], group, 2), query_x), "wloop")
        query_z = swapped(after(query_x, value_z), "seq")
        output_y = swapped(after(output_x, value_y), "groups")
        blocks = [
            (own[0], key_x, key_y),
            (own[1], value_half, after(value_y, query_x)),
            (own[2], query_x, after(query_z, output_x)),
        ]
    else:
        place = place_query = jnp.zeros((2,), jnp.int32)
        blocks = []
        for block in own[:3]:
            full = lax.all_gather(block, "wloop", axis=0, tiled=True)
            half = full.shape[0] // 2
            blocks.append((full[:half], full[half : half + half // 2], full[half + half // 2 :]))

    theirs = around(ours, "heads")
    prior = jnp.concatenate(
        [jnp.where(core == 0, ours, theirs), jnp.where(core == 0, theirs, ours)], axis=1
    )
    both = jnp.concatenate([prior, normed], axis=0)
    keys = projection(place, both, *blocks[0], head_dim)
    values = projection(place, both, *blocks[1], 0)
    queries = projection(place_query, normed, *blocks[2], head_dim)

    keep = (1 - resets[0, 0]).astype(F32)
    upto = jnp.triu(jnp.ones((span, span), F32))
    climb = jnp.dot(log_retain[0], upto, precision=lax.Precision.HIGHEST)
    whole = climb[:, -1]
    factor = jnp.exp(whole) * keep
    weight = jnp.exp(whole[:, None] - climb)
    local_state = local_states(keys, values, weight.T, head_dim)
    small = jnp.stack([*two_parts(factor), *two_parts(jnp.sum(weight * weight, axis=-1))], axis=1)
    small = jnp.pad(small, ((0, 0), (0, 12)))
    small = jnp.broadcast_to(small[:, :, None], (heads_here, 16, head_dim))
    gathered = lax.all_gather(jnp.concatenate([local_state, small], axis=1), "seq")
    state, mass = jnp.zeros(local_state.shape, F32), jnp.zeros(factor.shape, F32)
    for j in range(segments - 1):
        tail = gathered[j, :, head_dim : head_dim + 4, 0].astype(F32)
        fac, add_mass = tail[:, 0] + tail[:, 1], tail[:, 2] + tail[:, 3]
        past = j < seg
        local = gathered[j, :, :head_dim].astype(F32)
        state = jnp.where(past, fac[:, None, None] * state + local, state)
        mass = jnp.where(past, fac * fac * mass + add_mass, mass)
    entering = (state * keep).astype(BF16)
    decay = jnp.exp(climb) / jnp.sqrt(head_dim * (1.0 + mass * keep))[:, None]
    allow = ((keep > 0.5) & (seg > 0)).astype(F32).reshape(1, 1)
    window = window_mix(queries, keys, values, allow, head_dim, scale)
    attended = add_read(queries, entering, decay.T, window)

    if paired:
        other = in_order(group, output_x, output_y)
        mine = jnp.where(side == core, w_output, other)
        theirs = jnp.where(side == core, other, w_output)
    else:
        full = lax.all_gather(w_output, "wloop", axis=1, tiled=True)
        share = width // 2
        mine = lax.dynamic_slice_in_dim(full, core * share, share, 1)
        theirs = lax.dynamic_slice_in_dim(full, (1 - core) * share, share, 1)
    sent = around(jnp.dot(attended, theirs, preferred_element_type=F32).astype(BF16), "heads")
    share = mine.shape[1]
    summed = jnp.dot(attended, mine, preferred_element_type=F32) + sent.astype(F32)
    residual = lax.dynamic_slice_in_dim(acts, core * share, share, 1)
    return (residual.astype(F32) + summed).astype(BF16).reshape(trajs, span, share)


def solution(mesh):
    placed = (
        P(("groups", "wloop"), "seq", None),
        P(),
        P("wloop", "heads"),
        P("wloop", None, "heads"),
        P("heads", "wloop"),
        P(("groups", "wloop"), "heads", "seq"),
        P(("groups", "wloop"), "seq"),
    )
    return jax.shard_map(
        shards,
        mesh=mesh,
        in_specs=placed,
        out_specs=P(("groups", "wloop"), "seq", "heads"),
        check_vma=False,
    )
```

```python
import functools
import math

import jax
import jax.numpy as jnp
from jax import lax
from jax.experimental import pallas as pl
from jax.experimental.pallas import tpu as pltpu
from jax.sharding import PartitionSpec as P

SCORE_SCALE = 2.0
F32, BF16 = jnp.float32, jnp.bfloat16


def around(value, axis):
    count = lax.axis_size(axis)
    return lax.ppermute(value, axis, [(i, (i + 1) % count) for i in range(count)])


def shifted(value, axis):
    count = lax.axis_size(axis)
    return lax.ppermute(value, axis, [(i, i + 1) for i in range(count - 1)])


def rms_rows(values, eps):
    return values * lax.rsqrt(jnp.mean(values * values, axis=-1, keepdims=True) + eps)


def after(value, *earlier):
    return lax.optimization_barrier((value, *earlier))[0]


def part_of(block, index, count):
    rows = block.shape[0] // count
    return lax.dynamic_slice_in_dim(block, index * rows, rows, 0)


def swapped(value, axis):
    count = lax.axis_size(axis)
    return lax.ppermute(value, axis, [(i, i + 1 - 2 * (i % 2)) for i in range(count)])


def in_order(index, first, second):
    return jnp.concatenate(
        [jnp.where(index == 0, first, second), jnp.where(index == 0, second, first)], axis=0
    )


def projection_kernel(head_dim, place_ref, own_ref, first_ref, second_ref, *refs):
    out_ref = refs[-1]
    side, group = place_ref[0], place_ref[1]
    deep, part = own_ref.shape[0], first_ref.shape[0]
    base = (1 - side) * deep
    row = 0
    for x_ref in refs[:-1]:

        def product(start, w_ref):
            columns = x_ref[:, pl.ds(pl.multiple_of(start, 128), w_ref.shape[0])]
            return jnp.dot(columns, w_ref[...], preferred_element_type=F32)

        total = product(side * deep, own_ref)
        total += product(base + group * part, first_ref)
        total += product(base + (1 - group) * part, second_ref)
        there = slice(row, row + x_ref.shape[0])
        row += x_ref.shape[0]
        if not head_dim:
            out_ref[there, :] = total.astype(BF16)
            continue
        for start in range(0, total.shape[1], head_dim):
            head = total[:, start : start + head_dim]
            out_ref[there, start : start + head_dim] = rms_rows(head, 1e-06).astype(BF16)


def projection(place, rows, own, first, second, head_dim):
    width = rows[0].shape[1]
    count = sum(block.shape[0] for block in rows)
    inner = own.shape[1]
    tile = 256
    return pl.pallas_call(
        functools.partial(projection_kernel, head_dim),
        grid=(inner // tile,),
        in_specs=[
            pl.BlockSpec(memory_space=pltpu.SMEM),
            pl.BlockSpec((own.shape[0], tile), lambda c: (0, c)),
            pl.BlockSpec((first.shape[0], tile), lambda c: (0, c)),
            pl.BlockSpec((second.shape[0], tile), lambda c: (0, c)),
        ]
        + [pl.BlockSpec(block.shape, lambda c: (0, 0)) for block in rows],
        out_specs=pl.BlockSpec((count, tile), lambda c: (0, c)),
        out_shape=jax.ShapeDtypeStruct((count, inner), BF16),
        compiler_params=pltpu.CompilerParams(vmem_limit_bytes=32 << 20),
        cost_estimate=pl.CostEstimate(
            flops=2 * count * width * inner,
            bytes_accessed=2 * (count * width + width * inner + count * inner),
            transcendentals=0,
        ),
    )(place, own, first, second, *rows)


def head_column(values, head):
    column = lax.broadcasted_iota(jnp.int32, values.shape, 1)
    return jnp.sum(jnp.where(column == head, values, 0.0), axis=-1, keepdims=True)


def state_kernel(k_ref, v_ref, weight_ref, out_ref):
    count, head_dim = out_ref.shape[:2]
    weight = weight_ref[...]
    for h in range(count):
        mine = head_column(weight, pl.program_id(0) * count + h)
        here = slice(h * head_dim, (h + 1) * head_dim)
        faded = (k_ref[:, here].astype(F32) * mine).astype(BF16)
        out_ref[h] = lax.dot_general(
            faded, v_ref[:, here], (((0,), (0,)), ((), ())), preferred_element_type=F32
        ).astype(BF16)


def local_states(keys, values, weight, head_dim):
    span, heads = weight.shape
    step = math.gcd(heads, 4)
    block = pl.BlockSpec((span, step * head_dim), lambda h: (1, h))
    return pl.pallas_call(
        state_kernel,
        grid=(heads // step,),
        in_specs=[block, block, pl.BlockSpec((span, heads), lambda h: (0, 0))],
        out_specs=pl.BlockSpec((step, head_dim, head_dim), lambda h: (h, 0, 0)),
        out_shape=jax.ShapeDtypeStruct((heads, head_dim, head_dim), BF16),
    )(keys, values, weight)


def two_parts(value):
    high = value.astype(BF16)
    return high, (value - high.astype(F32)).astype(BF16)


def window_kernel(scale, allow_ref, q_ref, k_ref, v_ref, out_ref):
    span = q_ref.shape[0]
    query = q_ref[...]
    product = functools.partial(
        lax.dot_general, dimension_numbers=(((1,), (1,)), ((), ())), preferred_element_type=F32
    )
    prior = product(query, k_ref[:span, :])
    own = product(query, k_ref[span:, :])
    lower = lax.broadcasted_iota(jnp.int32, (span, span), 1) <= lax.broadcasted_iota(
        jnp.int32, (span, span), 0
    )
    weight = jnp.exp(jnp.where(lower, own, prior) * scale)
    own_w = jnp.where(lower, weight, 0.0)
    prior_w = jnp.where(lower, 0.0, weight) * allow_ref[0, 0]
    total = jnp.sum(own_w + prior_w, axis=-1, keepdims=True)
    mixed = jnp.dot(own_w.astype(BF16), v_ref[span:, :], preferred_element_type=F32)
    mixed += jnp.dot(prior_w.astype(BF16), v_ref[:span, :], preferred_element_type=F32)
    out_ref[...] = mixed / total


def window_mix(queries, keys, values, allow, head_dim, scale):
    span, inner = queries.shape
    return pl.pallas_call(
        functools.partial(window_kernel, scale),
        grid=(inner // head_dim,),
        in_specs=[
            pl.BlockSpec(memory_space=pltpu.SMEM),
            pl.BlockSpec((span, head_dim), lambda h: (0, h)),
            pl.BlockSpec((2 * span, head_dim), lambda h: (0, h)),
            pl.BlockSpec((2 * span, head_dim), lambda h: (0, h)),
        ],
        out_specs=pl.BlockSpec((span, head_dim), lambda h: (0, h)),
        out_shape=jax.ShapeDtypeStruct((span, inner), F32),
        compiler_params=pltpu.CompilerParams(vmem_limit_bytes=32 << 20),
        cost_estimate=pl.CostEstimate(
            flops=8 * span * span * inner, bytes_accessed=14 * span * inner, transcendentals=0
        ),
    )(allow, queries, keys, values)


def read_kernel(q_ref, state_ref, decay_ref, window_ref, out_ref):
    count, head_dim = state_ref.shape[:2]
    decay = decay_ref[...]
    for h in range(count):
        mine = head_column(decay, pl.program_id(0) * count + h)
        here = slice(h * head_dim, (h + 1) * head_dim)
        read = jnp.dot(q_ref[:, here], state_ref[h], preferred_element_type=F32)
        out_ref[:, here] = (window_ref[:, here] + mine * read).astype(BF16)


def add_read(queries, states, decay, window):
    span, inner = queries.shape
    heads, head_dim = states.shape[:2]
    step = math.gcd(heads, 4)
    block = pl.BlockSpec((span, step * head_dim), lambda h: (0, h))
    return pl.pallas_call(
        read_kernel,
        grid=(heads // step,),
        in_specs=[
            block,
            pl.BlockSpec((step, head_dim, head_dim), lambda h: (h, 0, 0)),
            pl.BlockSpec((span, heads), lambda h: (0, 0)),
            block,
        ],
        out_specs=block,
        out_shape=jax.ShapeDtypeStruct((span, inner), BF16),
    )(queries, states, decay, window)


def shards(activations, norm_gain, w_query, w_keyvalue, w_output, log_retain, resets):
    trajs, span, width = activations.shape
    heads_here = log_retain.shape[1]
    inner_here = w_query.shape[1]
    head_dim = inner_here // heads_here
    scale = SCORE_SCALE / math.sqrt(head_dim)
    side, core, seg = lax.axis_index("wloop"), lax.axis_index("heads"), lax.axis_index("seq")
    segments = lax.axis_size("seq")
    paired = lax.axis_size("wloop") == 2 and lax.axis_size("groups") == 2
    paired = paired and segments % 2 == 0
    acts = activations.reshape(span, width)

    group, twin = lax.axis_index("groups"), seg % 2
    place = jnp.stack([side, group]).astype(jnp.int32)
    place_query = jnp.stack([side, twin]).astype(jnp.int32)
    normed = (rms_rows(acts.astype(F32), 1e-05) * norm_gain).astype(BF16)
    lane = width // 2
    ours = shifted(lax.dynamic_slice_in_dim(normed, core * lane, lane, 1), "seq")
    w_pair = w_keyvalue.reshape(w_keyvalue.shape[0], 2 * inner_here)
    own = [w_pair[:, :inner_here], w_pair[:, inner_here:], w_query, w_output]
    if paired:
        key_x = swapped(part_of(own[0], group, 2), "wloop")
        key_y = swapped(key_x, "groups")
        value_x = swapped(after(part_of(own[1], 2 * group + twin, 4), key_x), "wloop")
        query_x = swapped(after(part_of(own[2], twin, 2), value_x), "wloop")
        value_z = swapped(after(value_x, ours), "seq")
        value_half = in_order(twin, value_x, value_z)
        value_y = swapped(after(value_half, key_y), "groups")
        output_x = swapped(after(part_of(own[3], group, 2), query_x), "wloop")
        query_z = swapped(after(query_x, value_z), "seq")
        output_y = swapped(after(output_x, value_y), "groups")
        blocks = [
            (own[0], key_x, key_y),
            (own[1], value_half, after(value_y, query_x)),
            (own[2], query_x, after(query_z, output_x)),
        ]
    else:
        place = place_query = jnp.zeros((2,), jnp.int32)
        blocks = []
        for block in own[:3]:
            full = lax.all_gather(block, "wloop", axis=0, tiled=True)
            half = full.shape[0] // 2
            blocks.append((full[:half], full[half : half + half // 2], full[half + half // 2 :]))

    theirs = around(ours, "heads")
    prior = jnp.concatenate(
        [jnp.where(core == 0, ours, theirs), jnp.where(core == 0, theirs, ours)], axis=1
    )
    both = (prior, normed)
    keys = projection(place, both, *blocks[0], head_dim)
    values = projection(place, both, *blocks[1], 0)
    queries = projection(place_query, (normed,), *blocks[2], head_dim)

    keep = (1 - resets[0, 0]).astype(F32)
    upto = jnp.triu(jnp.ones((span, span), F32))
    climb = jnp.dot(log_retain[0], upto, precision=lax.Precision.HIGHEST)
    whole = climb[:, -1]
    factor = jnp.exp(whole) * keep
    weight = jnp.exp(whole[:, None] - climb)
    local_state = local_states(keys, values, weight.T, head_dim)
    small = jnp.stack([*two_parts(factor), *two_parts(jnp.sum(weight * weight, axis=-1))], axis=1)
    small = jnp.pad(small, ((0, 0), (0, 12)))
    small = jnp.broadcast_to(small[:, :, None], (heads_here, 16, head_dim))
    gathered = lax.all_gather(jnp.concatenate([local_state, small], axis=1), "seq")
    state, mass = jnp.zeros(local_state.shape, F32), jnp.zeros(factor.shape, F32)
    for j in range(segments - 1):
        tail = gathered[j, :, head_dim : head_dim + 4, 0].astype(F32)
        fac, add_mass = tail[:, 0] + tail[:, 1], tail[:, 2] + tail[:, 3]
        past = j < seg
        local = gathered[j, :, :head_dim].astype(F32)
        state = jnp.where(past, fac[:, None, None] * state + local, state)
        mass = jnp.where(past, fac * fac * mass + add_mass, mass)
    entering = (state * keep).astype(BF16)
    decay = jnp.exp(climb) / jnp.sqrt(head_dim * (1.0 + mass * keep))[:, None]
    allow = ((keep > 0.5) & (seg > 0)).astype(F32).reshape(1, 1)
    window = window_mix(queries, keys, values, allow, head_dim, scale)
    attended = add_read(queries, entering, decay.T, window)

    if paired:
        other = in_order(group, output_x, output_y)
        mine = jnp.where(side == core, w_output, other)
        theirs = jnp.where(side == core, other, w_output)
    else:
        full = lax.all_gather(w_output, "wloop", axis=1, tiled=True)
        share = width // 2
        mine = lax.dynamic_slice_in_dim(full, core * share, share, 1)
        theirs = lax.dynamic_slice_in_dim(full, (1 - core) * share, share, 1)
    sent = around(jnp.dot(attended, theirs, preferred_element_type=F32).astype(BF16), "heads")
    share = mine.shape[1]
    summed = jnp.dot(attended, mine, preferred_element_type=F32) + sent.astype(F32)
    residual = lax.dynamic_slice_in_dim(acts, core * share, share, 1)
    return (residual.astype(F32) + summed).astype(BF16).reshape(trajs, span, share)


def solution(mesh):
    placed = (
        P(("groups", "wloop"), "seq", None),
        P(),
        P("wloop", "heads"),
        P("wloop", None, "heads"),
        P("heads", "wloop"),
        P(("groups", "wloop"), "heads", "seq"),
        P(("groups", "wloop"), "seq"),
    )
    return jax.shard_map(
        shards,
        mesh=mesh,
        in_specs=placed,
        out_specs=P(("groups", "wloop"), "seq", "heads"),
        check_vma=False,
    )
```

```python
import functools
import math

import jax
import jax.numpy as jnp
from jax import lax
from jax.experimental import pallas as pl
from jax.experimental.pallas import tpu as pltpu
from jax.sharding import PartitionSpec as P

SCORE_SCALE = 2.0
F32, BF16 = jnp.float32, jnp.bfloat16


def around(value, axis):
    count = lax.axis_size(axis)
    return lax.ppermute(value, axis, [(i, (i + 1) % count) for i in range(count)])


def shifted(value, axis):
    count = lax.axis_size(axis)
    return lax.ppermute(value, axis, [(i, i + 1) for i in range(count - 1)])


def rms_rows(values, eps):
    return values * lax.rsqrt(jnp.mean(values * values, axis=-1, keepdims=True) + eps)


def after(value, *earlier):
    return lax.optimization_barrier((value, *earlier))[0]


def part_of(block, index, count):
    rows = block.shape[0] // count
    return lax.dynamic_slice_in_dim(block, index * rows, rows, 0)


def swapped(value, axis):
    count = lax.axis_size(axis)
    return lax.ppermute(value, axis, [(i, i + 1 - 2 * (i % 2)) for i in range(count)])


def in_order(index, first, second):
    return jnp.concatenate(
        [jnp.where(index == 0, first, second), jnp.where(index == 0, second, first)], axis=0
    )


def projection_kernel(head_dim, place_ref, own_ref, first_ref, second_ref, *refs):
    out_ref = refs[-1]
    side, group = place_ref[0], place_ref[1]
    deep, part = own_ref.shape[0], first_ref.shape[0]
    base = (1 - side) * deep
    row = 0
    for x_ref in refs[:-1]:

        def product(start, w_ref):
            columns = x_ref[:, pl.ds(pl.multiple_of(start, 128), w_ref.shape[0])]
            return jnp.dot(columns, w_ref[...], preferred_element_type=F32)

        total = product(side * deep, own_ref)
        total += product(base + group * part, first_ref)
        total += product(base + (1 - group) * part, second_ref)
        there = slice(row, row + x_ref.shape[0])
        row += x_ref.shape[0]
        if not head_dim:
            out_ref[there, :] = total.astype(BF16)
            continue
        for start in range(0, total.shape[1], head_dim):
            head = total[:, start : start + head_dim]
            out_ref[there, start : start + head_dim] = rms_rows(head, 1e-06).astype(BF16)


def projection(place, rows, own, first, second, head_dim):
    width = rows[0].shape[1]
    count = sum(block.shape[0] for block in rows)
    inner = own.shape[1]
    tile = 256
    return pl.pallas_call(
        functools.partial(projection_kernel, head_dim),
        grid=(inner // tile,),
        in_specs=[
            pl.BlockSpec(memory_space=pltpu.SMEM),
            pl.BlockSpec((own.shape[0], tile), lambda c: (0, c)),
            pl.BlockSpec((first.shape[0], tile), lambda c: (0, c)),
            pl.BlockSpec((second.shape[0], tile), lambda c: (0, c)),
        ]
        + [pl.BlockSpec(block.shape, lambda c: (0, 0)) for block in rows],
        out_specs=pl.BlockSpec((count, tile), lambda c: (0, c)),
        out_shape=jax.ShapeDtypeStruct((count, inner), BF16),
        compiler_params=pltpu.CompilerParams(vmem_limit_bytes=32 << 20),
        cost_estimate=pl.CostEstimate(
            flops=2 * count * width * inner,
            bytes_accessed=2 * (count * width + width * inner + count * inner),
            transcendentals=0,
        ),
    )(place, own, first, second, *rows)


def head_column(values, head):
    column = lax.broadcasted_iota(jnp.int32, values.shape, 1)
    return jnp.sum(jnp.where(column == head, values, 0.0), axis=-1, keepdims=True)


def state_kernel(k_ref, v_ref, weight_ref, out_ref):
    count, head_dim = out_ref.shape[:2]
    weight = weight_ref[...]
    for h in range(count):
        mine = head_column(weight, pl.program_id(0) * count + h)
        here = slice(h * head_dim, (h + 1) * head_dim)
        faded = (k_ref[:, here].astype(F32) * mine).astype(BF16)
        out_ref[h] = lax.dot_general(
            faded, v_ref[:, here], (((0,), (0,)), ((), ())), preferred_element_type=F32
        ).astype(BF16)


def local_states(keys, values, weight, head_dim):
    span, heads = weight.shape
    step = math.gcd(heads, 4)
    block = pl.BlockSpec((span, step * head_dim), lambda h: (1, h))
    return pl.pallas_call(
        state_kernel,
        grid=(heads // step,),
        in_specs=[block, block, pl.BlockSpec((span, heads), lambda h: (0, 0))],
        out_specs=pl.BlockSpec((step, head_dim, head_dim), lambda h: (h, 0, 0)),
        out_shape=jax.ShapeDtypeStruct((heads, head_dim, head_dim), BF16),
    )(keys, values, weight)


def two_parts(value):
    high = value.astype(BF16)
    return high, (value - high.astype(F32)).astype(BF16)


def window_kernel(scale, allow_ref, q_ref, k_ref, v_ref, out_ref):
    span = q_ref.shape[0]
    query = q_ref[...]
    product = functools.partial(
        lax.dot_general, dimension_numbers=(((1,), (1,)), ((), ())), preferred_element_type=F32
    )
    prior = product(query, k_ref[:span, :])
    own = product(query, k_ref[span:, :])
    lower = lax.broadcasted_iota(jnp.int32, (span, span), 1) <= lax.broadcasted_iota(
        jnp.int32, (span, span), 0
    )
    weight = jnp.exp(jnp.where(lower, own, prior) * scale)
    own_w = jnp.where(lower, weight, 0.0)
    prior_w = jnp.where(lower, 0.0, weight) * allow_ref[0, 0]
    total = jnp.sum(own_w + prior_w, axis=-1, keepdims=True)
    mixed = jnp.dot(own_w.astype(BF16), v_ref[span:, :], preferred_element_type=F32)
    mixed += jnp.dot(prior_w.astype(BF16), v_ref[:span, :], preferred_element_type=F32)
    out_ref[...] = mixed / total


def window_mix(queries, keys, values, allow, head_dim, scale):
    span, inner = queries.shape
    return pl.pallas_call(
        functools.partial(window_kernel, scale),
        grid=(inner // head_dim,),
        in_specs=[
            pl.BlockSpec(memory_space=pltpu.SMEM),
            pl.BlockSpec((span, head_dim), lambda h: (0, h)),
            pl.BlockSpec((2 * span, head_dim), lambda h: (0, h)),
            pl.BlockSpec((2 * span, head_dim), lambda h: (0, h)),
        ],
        out_specs=pl.BlockSpec((span, head_dim), lambda h: (0, h)),
        out_shape=jax.ShapeDtypeStruct((span, inner), F32),
        compiler_params=pltpu.CompilerParams(vmem_limit_bytes=32 << 20),
        cost_estimate=pl.CostEstimate(
            flops=8 * span * span * inner, bytes_accessed=14 * span * inner, transcendentals=0
        ),
    )(allow, queries, keys, values)


def read_kernel(q_ref, state_ref, decay_ref, window_ref, out_ref):
    count, head_dim = state_ref.shape[:2]
    decay = decay_ref[...]
    for h in range(count):
        mine = head_column(decay, pl.program_id(0) * count + h)
        here = slice(h * head_dim, (h + 1) * head_dim)
        read = jnp.dot(q_ref[:, here], state_ref[h], preferred_element_type=F32)
        out_ref[:, here] = (window_ref[:, here] + mine * read).astype(BF16)


def add_read(queries, states, decay, window):
    span, inner = queries.shape
    heads, head_dim = states.shape[:2]
    step = math.gcd(heads, 4)
    block = pl.BlockSpec((span, step * head_dim), lambda h: (0, h))
    return pl.pallas_call(
        read_kernel,
        grid=(heads // step,),
        in_specs=[
            block,
            pl.BlockSpec((step, head_dim, head_dim), lambda h: (h, 0, 0)),
            pl.BlockSpec((span, heads), lambda h: (0, 0)),
            block,
        ],
        out_specs=block,
        out_shape=jax.ShapeDtypeStruct((span, inner), BF16),
    )(queries, states, decay, window)


def shards(activations, norm_gain, w_query, w_keyvalue, w_output, log_retain, resets):
    trajs, span, width = activations.shape
    heads_here = log_retain.shape[1]
    inner_here = w_query.shape[1]
    head_dim = inner_here // heads_here
    scale = SCORE_SCALE / math.sqrt(head_dim)
    side, core, seg = lax.axis_index("wloop"), lax.axis_index("heads"), lax.axis_index("seq")
    segments = lax.axis_size("seq")
    paired = lax.axis_size("wloop") == 2 and lax.axis_size("groups") == 2
    paired = paired and segments % 2 == 0
    acts = activations.reshape(span, width)

    group, twin = lax.axis_index("groups"), seg % 2
    place = jnp.stack([side, group]).astype(jnp.int32)
    place_query = jnp.stack([side, twin]).astype(jnp.int32)
    normed = (rms_rows(acts.astype(F32), 1e-05) * norm_gain).astype(BF16)
    lane = width // 2
    ours = shifted(lax.dynamic_slice_in_dim(normed, core * lane, lane, 1), "seq")
    theirs = around(ours, "heads")
    prior = jnp.concatenate(
        [jnp.where(core == 0, ours, theirs), jnp.where(core == 0, theirs, ours)], axis=1
    )
    both = (prior, normed)
    w_pair = w_keyvalue.reshape(w_keyvalue.shape[0], 2 * inner_here)
    own = [w_pair[:, :inner_here], w_pair[:, inner_here:], w_query, w_output]
    if paired:
        key_x = swapped(part_of(w_keyvalue, group, 2)[:, 0, :], "wloop")
        key_y = swapped(key_x, "groups")
        value_x = swapped(after(part_of(w_keyvalue, 2 * group + twin, 4)[:, 1, :], key_x), "wloop")
        query_x = swapped(after(part_of(own[2], twin, 2), value_x), "wloop")
        value_z = swapped(after(value_x, ours), "seq")
        value_half = in_order(twin, value_x, value_z)
        value_y = swapped(after(value_half, key_y), "groups")
        keys = projection(place, both, own[0], key_x, key_y, head_dim)
        query_x = after(query_x, keys)
        output_x = swapped(after(part_of(own[3], group, 2), query_x), "wloop")
        query_z = swapped(after(query_x, value_z), "seq")
        output_y = swapped(after(output_x, value_y), "groups")
        blocks = [
            (own[1], value_half, after(value_y, query_x)),
            (own[2], query_x, after(query_z, output_x)),
        ]
    else:
        place = place_query = jnp.zeros((2,), jnp.int32)
        blocks = []
        for block in own[:3]:
            full = lax.all_gather(block, "wloop", axis=0, tiled=True)
            half = full.shape[0] // 2
            blocks.append((full[:half], full[half : half + half // 2], full[half + half // 2 :]))

        keys = projection(place, both, *blocks[0], head_dim)
        blocks = blocks[1:]
    values = projection(place, both, *blocks[0], 0)
    queries = projection(place_query, (normed,), *blocks[1], head_dim)

    keep = (1 - resets[0, 0]).astype(F32)
    upto = jnp.triu(jnp.ones((span, span), F32))
    climb = jnp.dot(log_retain[0], upto, precision=lax.Precision.HIGHEST)
    whole = climb[:, -1]
    factor = jnp.exp(whole) * keep
    weight = jnp.exp(whole[:, None] - climb)
    local_state = local_states(keys, values, weight.T, head_dim)
    small = jnp.stack([*two_parts(factor), *two_parts(jnp.sum(weight * weight, axis=-1))], axis=1)
    small = jnp.pad(small, ((0, 0), (0, 12)))
    small = jnp.broadcast_to(small[:, :, None], (heads_here, 16, head_dim))
    gathered = lax.all_gather(jnp.concatenate([local_state, small], axis=1), "seq")
    state, mass = jnp.zeros(local_state.shape, F32), jnp.zeros(factor.shape, F32)
    for j in range(segments - 1):
        tail = gathered[j, :, head_dim : head_dim + 4, 0].astype(F32)
        fac, add_mass = tail[:, 0] + tail[:, 1], tail[:, 2] + tail[:, 3]
        past = j < seg
        local = gathered[j, :, :head_dim].astype(F32)
        state = jnp.where(past, fac[:, None, None] * state + local, state)
        mass = jnp.where(past, fac * fac * mass + add_mass, mass)
    entering = (state * keep).astype(BF16)
    decay = jnp.exp(climb) / jnp.sqrt(head_dim * (1.0 + mass * keep))[:, None]
    allow = ((keep > 0.5) & (seg > 0)).astype(F32).reshape(1, 1)
    window = window_mix(queries, keys, values, allow, head_dim, scale)
    attended = add_read(queries, entering, decay.T, window)

    if paired:
        other = in_order(group, output_x, output_y)
        mine = jnp.where(side == core, w_output, other)
        theirs = jnp.where(side == core, other, w_output)
    else:
        full = lax.all_gather(w_output, "wloop", axis=1, tiled=True)
        share = width // 2
        mine = lax.dynamic_slice_in_dim(full, core * share, share, 1)
        theirs = lax.dynamic_slice_in_dim(full, (1 - core) * share, share, 1)
    sent = around(jnp.dot(attended, theirs, preferred_element_type=F32).astype(BF16), "heads")
    share = mine.shape[1]
    summed = jnp.dot(attended, mine, preferred_element_type=F32) + sent.astype(F32)
    residual = lax.dynamic_slice_in_dim(acts, core * share, share, 1)
    return (residual.astype(F32) + summed).astype(BF16).reshape(trajs, span, share)


def solution(mesh):
    placed = (
        P(("groups", "wloop"), "seq", None),
        P(),
        P("wloop", "heads"),
        P("wloop", None, "heads"),
        P("heads", "wloop"),
        P(("groups", "wloop"), "heads", "seq"),
        P(("groups", "wloop"), "seq"),
    )
    return jax.shard_map(
        shards,
        mesh=mesh,
        in_specs=placed,
        out_specs=P(("groups", "wloop"), "seq", "heads"),
        check_vma=False,
    )
```

```python
import functools
import math

import jax
import jax.numpy as jnp
from jax import lax
from jax.experimental import pallas as pl
from jax.experimental.pallas import tpu as pltpu
from jax.sharding import PartitionSpec as P

SCORE_SCALE = 2.0
F32, BF16 = jnp.float32, jnp.bfloat16


def around(value, axis):
    count = lax.axis_size(axis)
    return lax.ppermute(value, axis, [(i, (i + 1) % count) for i in range(count)])


def shifted(value, axis):
    count = lax.axis_size(axis)
    return lax.ppermute(value, axis, [(i, i + 1) for i in range(count - 1)])


def rms_rows(values, eps):
    return values * lax.rsqrt(jnp.mean(values * values, axis=-1, keepdims=True) + eps)


def after(value, *earlier):
    return lax.optimization_barrier((value, *earlier))[0]


def part_of(block, index, count):
    rows = block.shape[0] // count
    return lax.dynamic_slice_in_dim(block, index * rows, rows, 0)


def swapped(value, axis):
    count = lax.axis_size(axis)
    return lax.ppermute(value, axis, [(i, i + 1 - 2 * (i % 2)) for i in range(count)])


def in_order(index, first, second):
    return jnp.concatenate(
        [jnp.where(index == 0, first, second), jnp.where(index == 0, second, first)], axis=0
    )


def projection_kernel(head_dim, place_ref, own_ref, first_ref, second_ref, *refs):
    out_ref = refs[-1]
    side, group = place_ref[0], place_ref[1]
    deep, part = own_ref.shape[0], first_ref.shape[0]
    base = (1 - side) * deep
    row = 0
    for x_ref in refs[:-1]:

        def product(start, w_ref):
            columns = x_ref[:, pl.ds(pl.multiple_of(start, 128), w_ref.shape[0])]
            return jnp.dot(columns, w_ref[...], preferred_element_type=F32)

        total = product(side * deep, own_ref)
        total += product(base + group * part, first_ref)
        total += product(base + (1 - group) * part, second_ref)
        there = slice(row, row + x_ref.shape[0])
        row += x_ref.shape[0]
        if not head_dim:
            out_ref[there, :] = total.astype(BF16)
            continue
        for start in range(0, total.shape[1], head_dim):
            head = total[:, start : start + head_dim]
            out_ref[there, start : start + head_dim] = rms_rows(head, 1e-06).astype(BF16)


def projection(place, rows, own, first, second, head_dim):
    width = rows[0].shape[1]
    count = sum(block.shape[0] for block in rows)
    inner = own.shape[1]
    tile = 256
    return pl.pallas_call(
        functools.partial(projection_kernel, head_dim),
        grid=(inner // tile,),
        in_specs=[
            pl.BlockSpec(memory_space=pltpu.SMEM),
            pl.BlockSpec((own.shape[0], tile), lambda c: (0, c)),
            pl.BlockSpec((first.shape[0], tile), lambda c: (0, c)),
            pl.BlockSpec((second.shape[0], tile), lambda c: (0, c)),
        ]
        + [pl.BlockSpec(block.shape, lambda c: (0, 0)) for block in rows],
        out_specs=pl.BlockSpec((count, tile), lambda c: (0, c)),
        out_shape=jax.ShapeDtypeStruct((count, inner), BF16),
        compiler_params=pltpu.CompilerParams(vmem_limit_bytes=32 << 20),
        cost_estimate=pl.CostEstimate(
            flops=2 * count * width * inner,
            bytes_accessed=2 * (count * width + width * inner + count * inner),
            transcendentals=0,
        ),
    )(place, own, first, second, *rows)


def head_column(values, head):
    column = lax.broadcasted_iota(jnp.int32, values.shape, 1)
    return jnp.sum(jnp.where(column == head, values, 0.0), axis=-1, keepdims=True)


def state_kernel(k_ref, v_ref, weight_ref, out_ref):
    count, head_dim = out_ref.shape[:2]
    weight = weight_ref[...]
    for h in range(count):
        mine = head_column(weight, pl.program_id(0) * count + h)
        here = slice(h * head_dim, (h + 1) * head_dim)
        faded = (k_ref[:, here].astype(F32) * mine).astype(BF16)
        out_ref[h] = lax.dot_general(
            faded, v_ref[:, here], (((0,), (0,)), ((), ())), preferred_element_type=F32
        ).astype(BF16)


def local_states(keys, values, weight, head_dim):
    span, heads = weight.shape
    step = math.gcd(heads, 4)
    block = pl.BlockSpec((span, step * head_dim), lambda h: (1, h))
    return pl.pallas_call(
        state_kernel,
        grid=(heads // step,),
        in_specs=[block, block, pl.BlockSpec((span, heads), lambda h: (0, 0))],
        out_specs=pl.BlockSpec((step, head_dim, head_dim), lambda h: (h, 0, 0)),
        out_shape=jax.ShapeDtypeStruct((heads, head_dim, head_dim), BF16),
    )(keys, values, weight)


def two_parts(value):
    high = value.astype(BF16)
    return high, (value - high.astype(F32)).astype(BF16)


def window_kernel(scale, allow_ref, q_ref, k_ref, v_ref, out_ref):
    span = q_ref.shape[0]
    query = q_ref[...]
    product = functools.partial(
        lax.dot_general, dimension_numbers=(((1,), (1,)), ((), ())), preferred_element_type=F32
    )
    prior = product(query, k_ref[:span, :])
    own = product(query, k_ref[span:, :])
    lower = lax.broadcasted_iota(jnp.int32, (span, span), 1) <= lax.broadcasted_iota(
        jnp.int32, (span, span), 0
    )
    weight = jnp.exp(jnp.where(lower, own, prior) * scale)
    own_w = jnp.where(lower, weight, 0.0)
    prior_w = jnp.where(lower, 0.0, weight) * allow_ref[0, 0]
    total = jnp.sum(own_w + prior_w, axis=-1, keepdims=True)
    mixed = jnp.dot(own_w.astype(BF16), v_ref[span:, :], preferred_element_type=F32)
    mixed += jnp.dot(prior_w.astype(BF16), v_ref[:span, :], preferred_element_type=F32)
    out_ref[...] = mixed / total


def window_mix(queries, keys, values, allow, head_dim, scale):
    span, inner = queries.shape
    return pl.pallas_call(
        functools.partial(window_kernel, scale),
        grid=(inner // head_dim,),
        in_specs=[
            pl.BlockSpec(memory_space=pltpu.SMEM),
            pl.BlockSpec((span, head_dim), lambda h: (0, h)),
            pl.BlockSpec((2 * span, head_dim), lambda h: (0, h)),
            pl.BlockSpec((2 * span, head_dim), lambda h: (0, h)),
        ],
        out_specs=pl.BlockSpec((span, head_dim), lambda h: (0, h)),
        out_shape=jax.ShapeDtypeStruct((span, inner), F32),
        compiler_params=pltpu.CompilerParams(vmem_limit_bytes=32 << 20),
        cost_estimate=pl.CostEstimate(
            flops=8 * span * span * inner, bytes_accessed=14 * span * inner, transcendentals=0
        ),
    )(allow, queries, keys, values)


def read_kernel(q_ref, state_ref, decay_ref, window_ref, out_ref):
    count, head_dim = state_ref.shape[:2]
    decay = decay_ref[...]
    for h in range(count):
        mine = head_column(decay, pl.program_id(0) * count + h)
        here = slice(h * head_dim, (h + 1) * head_dim)
        read = jnp.dot(q_ref[:, here], state_ref[h], preferred_element_type=F32)
        out_ref[:, here] = (window_ref[:, here] + mine * read).astype(BF16)


def add_read(queries, states, decay, window):
    span, inner = queries.shape
    heads, head_dim = states.shape[:2]
    step = math.gcd(heads, 4)
    block = pl.BlockSpec((span, step * head_dim), lambda h: (0, h))
    return pl.pallas_call(
        read_kernel,
        grid=(heads // step,),
        in_specs=[
            block,
            pl.BlockSpec((step, head_dim, head_dim), lambda h: (h, 0, 0)),
            pl.BlockSpec((span, heads), lambda h: (0, 0)),
            block,
        ],
        out_specs=block,
        out_shape=jax.ShapeDtypeStruct((span, inner), BF16),
    )(queries, states, decay, window)


def shards(activations, norm_gain, w_query, w_keyvalue, w_output, log_retain, resets):
    trajs, span, width = activations.shape
    heads_here = log_retain.shape[1]
    inner_here = w_query.shape[1]
    head_dim = inner_here // heads_here
    scale = SCORE_SCALE / math.sqrt(head_dim)
    side, core, seg = lax.axis_index("wloop"), lax.axis_index("heads"), lax.axis_index("seq")
    segments = lax.axis_size("seq")
    paired = lax.axis_size("wloop") == 2 and lax.axis_size("groups") == 2
    paired = paired and segments % 2 == 0
    acts = activations.reshape(span, width)

    group, twin = lax.axis_index("groups"), seg % 2
    place = jnp.stack([side, group]).astype(jnp.int32)
    place_query = jnp.stack([side, twin]).astype(jnp.int32)
    normed = (rms_rows(acts.astype(F32), 1e-05) * norm_gain).astype(BF16)
    lane = width // 2
    ours = shifted(lax.dynamic_slice_in_dim(normed, core * lane, lane, 1), "seq")
    theirs = around(ours, "heads")
    prior = jnp.concatenate(
        [jnp.where(core == 0, ours, theirs), jnp.where(core == 0, theirs, ours)], axis=1
    )
    both = (prior, normed)
    w_pair = w_keyvalue.reshape(w_keyvalue.shape[0], 2 * inner_here)
    own = [w_pair[:, :inner_here], w_pair[:, inner_here:], w_query, w_output]
    if paired:
        key_x = swapped(part_of(w_keyvalue, group, 2)[:, 0, :], "wloop")
        value_part = part_of(w_keyvalue, 2 * group + twin, 4)[:, 1, :]
        query_part, output_part = part_of(w_query, twin, 2), part_of(w_output, group, 2)
        key_x, own[0], own[1], value_part, query_part, output_part = lax.optimization_barrier(
            (key_x, own[0], own[1], value_part, query_part, output_part)
        )
        key_y = swapped(key_x, "groups")
        value_x = swapped(value_part, "wloop")
        query_x = swapped(after(query_part, value_x), "wloop")
        value_z = swapped(after(value_x, ours), "seq")
        value_half = in_order(twin, value_x, value_z)
        value_y = swapped(after(value_half, key_y), "groups")
        keys = projection(place, both, own[0], key_x, key_y, head_dim)
        query_x = after(query_x, keys)
        output_x = swapped(after(output_part, query_x), "wloop")
        query_z = swapped(after(query_x, value_z), "seq")
        output_y = swapped(after(output_x, value_y), "groups")
        blocks = [
            (own[1], value_half, after(value_y, query_x)),
            (own[2], query_x, after(query_z, output_x)),
        ]
    else:
        place = place_query = jnp.zeros((2,), jnp.int32)
        blocks = []
        for block in own[:3]:
            full = lax.all_gather(block, "wloop", axis=0, tiled=True)
            half = full.shape[0] // 2
            blocks.append((full[:half], full[half : half + half // 2], full[half + half // 2 :]))

        keys = projection(place, both, *blocks[0], head_dim)
        blocks = blocks[1:]
    values = projection(place, both, *blocks[0], 0)
    queries = projection(place_query, (normed,), *blocks[1], head_dim)

    keep = (1 - resets[0, 0]).astype(F32)
    upto = jnp.triu(jnp.ones((span, span), F32))
    climb = jnp.dot(log_retain[0], upto, precision=lax.Precision.HIGHEST)
    whole = climb[:, -1]
    factor = jnp.exp(whole) * keep
    weight = jnp.exp(whole[:, None] - climb)
    local_state = local_states(keys, values, weight.T, head_dim)
    small = jnp.stack([*two_parts(factor), *two_parts(jnp.sum(weight * weight, axis=-1))], axis=1)
    small = jnp.pad(small, ((0, 0), (0, 12)))
    small = jnp.broadcast_to(small[:, :, None], (heads_here, 16, head_dim))
    gathered = lax.all_gather(jnp.concatenate([local_state, small], axis=1), "seq")
    state, mass = jnp.zeros(local_state.shape, F32), jnp.zeros(factor.shape, F32)
    for j in range(segments - 1):
        tail = gathered[j, :, head_dim : head_dim + 4, 0].astype(F32)
        fac, add_mass = tail[:, 0] + tail[:, 1], tail[:, 2] + tail[:, 3]
        past = j < seg
        local = gathered[j, :, :head_dim].astype(F32)
        state = jnp.where(past, fac[:, None, None] * state + local, state)
        mass = jnp.where(past, fac * fac * mass + add_mass, mass)
    entering = (state * keep).astype(BF16)
    decay = jnp.exp(climb) / jnp.sqrt(head_dim * (1.0 + mass * keep))[:, None]
    allow = ((keep > 0.5) & (seg > 0)).astype(F32).reshape(1, 1)
    window = window_mix(queries, keys, values, allow, head_dim, scale)
    attended = add_read(queries, entering, decay.T, window)

    if paired:
        other = in_order(group, output_x, output_y)
        mine = jnp.where(side == core, w_output, other)
        theirs = jnp.where(side == core, other, w_output)
    else:
        full = lax.all_gather(w_output, "wloop", axis=1, tiled=True)
        share = width // 2
        mine = lax.dynamic_slice_in_dim(full, core * share, share, 1)
        theirs = lax.dynamic_slice_in_dim(full, (1 - core) * share, share, 1)
    sent = around(jnp.dot(attended, theirs, preferred_element_type=F32).astype(BF16), "heads")
    share = mine.shape[1]
    summed = jnp.dot(attended, mine, preferred_element_type=F32) + sent.astype(F32)
    residual = lax.dynamic_slice_in_dim(acts, core * share, share, 1)
    return (residual.astype(F32) + summed).astype(BF16).reshape(trajs, span, share)


def solution(mesh):
    placed = (
        P(("groups", "wloop"), "seq", None),
        P(),
        P("wloop", "heads"),
        P("wloop", None, "heads"),
        P("heads", "wloop"),
        P(("groups", "wloop"), "heads", "seq"),
        P(("groups", "wloop"), "seq"),
    )
    return jax.shard_map(
        shards,
        mesh=mesh,
        in_specs=placed,
        out_specs=P(("groups", "wloop"), "seq", "heads"),
        check_vma=False,
    )
```
